32 devices in a mesh: row: 8 (over z, y), col: 2 (over x), layer: 2 (over core).
Axes of the slice: x: 2, y: 2, z: 4, core: 2. Of those that a mesh axis runs over, the one named last changes fastest.
Arguments:
- p_blocks: bfloat16 [128, 10, 128, 128], P('row', 'col'), may hold values from -1.1953125 to 1.1953125
- p_cols: int32 [128, 10], P('row', 'col'), may hold values from 0 to 127, as said below
- keep_cols: int32 [128, 24], P('row', 'col'), may hold values from -1 to 127, as said below
Outputs:
- purified: bfloat16 [128, 24, 128, 128], P(('row', 'layer'), 'col')
The draws below stay inside these ranges and needn't reach their ends.
Inputs may be any that keep to these rules, and one draw needn't show every extreme that they name: `p_cols`: slot s of a block row lies in column panel s // 5, where block column k belongs to panel (k mod 16) // 8. The columns of a block row are distinct, and every block row holds its own diagonal block. `keep_cols`: slots t of a block row for panel t // 12 hold distinct block columns of that panel, followed by -1 in the unused slots; each block row uses 2 or more slots of every panel, and the first block row of every index of row uses all 12 slots of every panel.
All inputs are finite; a program needn't handle non-finite values.
Results may differ from the reference program's by a relative error of at most 0.0048.
Values may be sent and summed in bfloat16 or wider, within the bound.
A program may use at most 320 MiB of HBM per device.

```python
import jax
import jax.numpy as jnp
from jax import lax

BLOCK = 128
ROWS_DEV = 16
SLOTS = 5
KEEP_SLOTS = 12
SUB_ROWS = 8
NBLK = 128
ALL_SLOTS = 10
N_ROW = 8
N_COL = 2


def pattern_parts(key):
    row_count = ROWS_DEV * N_ROW
    panel_width = row_count // N_COL
    sub_count = SUB_ROWS
    row_ids = jnp.arange(row_count, dtype=jnp.int32)
    position = jnp.arange(panel_width, dtype=jnp.int32)
    panel_ids = jnp.arange(N_COL, dtype=jnp.int32)
    column_of = position[None, :] // sub_count * ROWS_DEV + panel_ids[:, None] * sub_count + position[None, :] % sub_count
    scores = jax.random.randint(jax.random.fold_in(key, 11), (row_count, N_COL, panel_width), 0, 1 << 20, dtype=jnp.int32)
    scores = scores * panel_width + position[None, None, :]
    own_diag = column_of[None, :, :] == row_ids[:, None, None]
    scores = jnp.where(own_diag, -1, scores)
    ordering = jnp.argsort(scores, axis=-1, stable=True)
    chosen = jnp.take_along_axis(jnp.broadcast_to(column_of[None], (row_count, N_COL, panel_width)), ordering, axis=-1)
    counts = jax.random.randint(jax.random.fold_in(key, 12), (row_count, N_COL, 1), 2, KEEP_SLOTS + 1, dtype=jnp.int32)
    counts = jnp.where((row_ids % ROWS_DEV == 0)[:, None, None], KEEP_SLOTS, counts)
    return (chosen.astype(jnp.int32), counts)


def draw_p_cols(key, part):
    chosen, counts = pattern_parts(key)
    return chosen[:, :, :SLOTS].reshape((NBLK, N_COL * SLOTS))


def draw_keep_cols(key, part):
    chosen, counts = pattern_parts(key)
    slot_pos = jnp.arange(KEEP_SLOTS, dtype=jnp.int32)[None, None, :]
    kept = jnp.where(slot_pos < counts, chosen[:, :, :KEEP_SLOTS], -1)
    return kept.reshape((NBLK, N_COL * KEEP_SLOTS)).astype(jnp.int32)


def block_levels(own_key, extent, shards, smallest, largest):
    def one(axis_at, blocks):
        heights = jax.random.uniform(jax.random.fold_in(jax.random.fold_in(own_key, 6), axis_at), (blocks,), jnp.float32, smallest / len(shards), largest / len(shards))
        return jnp.repeat(jnp.exp(heights), extent[axis_at] // blocks).reshape((-1,) + (1,) * (len(extent) - axis_at - 1))

    factor_of = one(*shards[0])
    for cut in shards[1:]:
        factor_of = factor_of * one(*cut)
    return factor_of


def gaussian(own_key, shape, scale, bound, cuts=(), held_as=jnp.bfloat16):
    values = jax.random.normal(own_key, shape, jnp.float32) * scale
    if len(cuts) > 0:
        values = block_levels(own_key, shape, cuts, -0.22, 0.18) * values
    return jnp.clip(values, min=-bound, max=bound).astype(held_as)


def setup_inputs(seed: int = 0) -> dict:
    seeds = jax.random.split(jax.random.key(seed), 4)
    p_blocks = gaussian(seeds[0], (NBLK, ALL_SLOTS, BLOCK, BLOCK), 0.2, 1.1953125, ((0, 8), (1, 2)))
    p_cols = draw_p_cols(jax.random.fold_in(seeds[3], 71), 0)
    keep_cols = draw_keep_cols(jax.random.fold_in(seeds[3], 71), 0)
    return {"p_blocks": p_blocks, "p_cols": p_cols, "keep_cols": keep_cols}


def lookup_table(p_cols):
    row_count = p_cols.shape[0]
    slot_table = jnp.full((row_count, row_count), -1, jnp.int32)
    row_ids = jnp.broadcast_to(jnp.arange(row_count, dtype=jnp.int32)[:, None], p_cols.shape)
    slot_ids = jnp.broadcast_to(jnp.arange(p_cols.shape[1], dtype=jnp.int32)[None, :], p_cols.shape)
    return slot_table.at[row_ids, p_cols].set(slot_ids)


def filtered_product(left_blocks, left_cols, keep_cols, p_blocks, slot_table):
    def one_row(pieces):
        blocks, columns, wanted = pieces
        present = columns >= 0
        safe_cols = jnp.where(present, columns, 0).astype(jnp.int32)
        safe_want = jnp.where(wanted >= 0, wanted, 0).astype(jnp.int32)
        found_slot = slot_table[safe_cols[:, None], safe_want[None, :]]
        usable = (found_slot >= 0) & present[:, None] & (wanted >= 0)[None, :]
        picked = p_blocks[safe_cols[:, None], jnp.where(usable, found_slot, 0).astype(jnp.int32)]
        picked = jnp.where(usable[:, :, None, None], picked.astype(jnp.float32), jnp.float32(0.0))
        return jnp.einsum("axy,atyz->txz", blocks.astype(jnp.float32), picked)
    return lax.map(one_row, (left_blocks, left_cols, keep_cols))


def reference(p_blocks, p_cols, keep_cols):
    slot_table = lookup_table(p_cols)
    square = filtered_product(p_blocks, p_cols, keep_cols, p_blocks, slot_table)
    square_half = lax.optimization_barrier(square.astype(jnp.bfloat16))
    cube_sum = filtered_product(square_half, keep_cols, keep_cols, p_blocks, slot_table)
    return (3.0 * square - 2.0 * cube_sum).astype(jnp.bfloat16)
```

```python
import functools

import jax
import jax.numpy as jnp
from jax import lax
from jax.experimental import pallas as pl
from jax.experimental.pallas import tpu as pltpu
from jax.sharding import PartitionSpec as P

MESH = pl.DeviceIdType.MESH
LANES = 128
DEPTH = 16
GROUP = 4


def gather_kernel(
    n_row,
    lines,
    blocks_ref,
    meta_ref,
    full_ref,
    table_ref,
    other_ref,
    other_meta_ref,
    z_send,
    z_recv,
    y_send,
    y_recv,
    c_send,
    c_recv,
    m_send,
    m_recv,
    x_send,
    x_recv,
    local,
):
    row, col, layer = lax.axis_index("row"), lax.axis_index("col"), lax.axis_index("layer")
    length = n_row // 2
    z, y = row // 2, row % 2
    half = blocks_ref.shape[0] // 2
    mine = pl.ds(pl.multiple_of(layer * half, half), half)
    theirs = pl.ds(pl.multiple_of((1 - layer) * half, half), half)
    parts = len(lines)

    barrier = pltpu.get_barrier_semaphore()
    for step in range(1, n_row):
        pl.semaphore_signal(
            barrier, inc=1, device_id=(lax.rem(row + step, n_row), col, layer), device_id_type=MESH
        )
    pl.semaphore_signal(barrier, inc=1, device_id=(row, 1 - col, layer), device_id_type=MESH)
    pl.semaphore_signal(barrier, inc=1, device_id=(row, col, 1 - layer), device_id_type=MESH)
    pl.semaphore_wait(barrier, n_row + 1)

    def source(part, chunk):
        lo, hi = lines[part]
        if chunk is None:
            return blocks_ref.at[mine, pl.ds(lo, hi - lo)]
        return full_ref.at[chunk, mine, pl.ds(lo, hi - lo)]

    def target(part, chunk, rows):
        lo, hi = lines[part]
        return full_ref.at[chunk, rows, pl.ds(lo, hi - lo)]

    def z_copy(part, pos, way, own):
        chunk = pos * 2 + y
        return pltpu.make_async_remote_copy(
            src_ref=source(part, None if own else chunk),
            dst_ref=target(part, chunk, mine),
            send_sem=z_send.at[part, way, pos],
            recv_sem=z_recv.at[part, pos],
            device_id=(row + (2 if way else -2), col, layer),
            device_id_type=MESH,
        )

    def y_copy(part, pos, own, arriving=False):
        chunk = pos * 2 + (1 - y if arriving else y)
        return pltpu.make_async_remote_copy(
            src_ref=source(part, None if own else chunk),
            dst_ref=target(part, chunk, mine),
            send_sem=y_send.at[part, pos],
            recv_sem=y_recv.at[part, pos],
            device_id=(z * 2 + 1 - y, col, layer),
            device_id_type=MESH,
        )

    def c_copy(part, chunk, arriving=False):
        return pltpu.make_async_remote_copy(
            src_ref=source(part, chunk),
            dst_ref=target(part, chunk, theirs if arriving else mine),
            send_sem=c_send.at[part, chunk],
            recv_sem=c_recv.at[part, chunk],
            device_id=(row, col, 1 - layer),
            device_id_type=MESH,
        )

    def m_copy(step, arriving=False):
        return pltpu.make_async_remote_copy(
            src_ref=meta_ref,
            dst_ref=table_ref.at[lax.rem(row - step + n_row, n_row) if arriving else row],
            send_sem=m_send.at[step],
            recv_sem=m_recv.at[step],
            device_id=(lax.rem(row + step, n_row), col, layer),
            device_id_type=MESH,
        )

    x_block = pltpu.make_async_remote_copy(
        src_ref=blocks_ref.at[mine],
        dst_ref=other_ref,
        send_sem=x_send.at[0],
        recv_sem=x_recv.at[0],
        device_id=(row, 1 - col, layer),
        device_id_type=MESH,
    )
    x_meta = pltpu.make_async_remote_copy(
        src_ref=meta_ref,
        dst_ref=other_meta_ref,
        send_sem=x_send.at[1],
        recv_sem=x_recv.at[1],
        device_id=(row, 1 - col, layer),
        device_id_type=MESH,
    )

    def go_right(pos):
        return pl.when(z < length - 1)

    for part in range(parts):
        y_copy(part, z, True).start()

        @pl.when(z < length - 1)
        def _():
            z_copy(part, z, 1, True).start()

        @pl.when(z > 0)
        def _():
            z_copy(part, z, 0, True).start()

    x_block.start()
    x_meta.start()
    for step in range(1, n_row):
        m_copy(step).start()
    own_blocks = pltpu.make_async_copy(blocks_ref, full_ref.at[row], local.at[0])
    own_meta = pltpu.make_async_copy(meta_ref, table_ref.at[row], local.at[1])
    own_blocks.start()
    own_meta.start()

    def from_side(part, pos, way):
        z_copy(part, pos, way, False).wait_recv()
        y_copy(part, pos, False).start()

        @pl.when((z < length - 1) if way else (z > 0))
        def _():
            z_copy(part, pos, way, False).start()

        c_copy(part, pos * 2 + y).start()

    def from_y(part, pos):
        y_copy(part, pos, False, True).wait_recv()
        c_copy(part, pos * 2 + 1 - y).start()

    for step in range(1, length + 1):
        for part in range(parts):
            if step < length:

                @pl.when(z - step >= 0)
                def _():
                    from_side(part, z - step, 1)

                @pl.when(z + step < length)
                def _():
                    from_side(part, z + step, 0)

        for part in range(parts):
            if step == 1:
                from_y(part, z)
            else:

                @pl.when(z - step + 1 >= 0)
                def _():
                    from_y(part, z - step + 1)

                @pl.when(z + step - 1 < length)
                def _():
                    from_y(part, z + step - 1)

    for step in range(1, n_row):
        m_copy(step, True).wait_recv()
        m_copy(step).wait_send()
    x_block.wait()
    x_meta.wait()
    own_blocks.wait()
    own_meta.wait()

    for part in range(parts):
        for pos in range(length):
            y_copy(part, pos, False).wait_send()

            @pl.when((pos <= z) & (z < length - 1))
            def _():
                z_copy(part, pos, 1, False).wait_send()

            @pl.when((pos >= z) & (z > 0))
            def _():
                z_copy(part, pos, 0, False).wait_send()

        for chunk in range(n_row):

            @pl.when(chunk != row)
            def _():
                c_copy(part, chunk).wait_send()
                c_copy(part, chunk, True).wait_recv()


def gather(blocks, meta, n_row):
    rows, slots = blocks.shape[:2]
    middle = slots // 2
    lines = ((0, middle), (middle, slots))
    parts = len(lines)
    length = n_row // 2
    anywhere = pl.BlockSpec(memory_space=pl.ANY)
    dma = pltpu.SemaphoreType.DMA
    return pl.pallas_call(
        functools.partial(gather_kernel, n_row, lines),
        out_shape=(
            jax.ShapeDtypeStruct((n_row,) + blocks.shape, blocks.dtype),
            jax.ShapeDtypeStruct((n_row,) + meta.shape, meta.dtype),
            jax.ShapeDtypeStruct((rows // 2,) + blocks.shape[1:], blocks.dtype),
            jax.ShapeDtypeStruct(meta.shape, meta.dtype),
        ),
        in_specs=[anywhere] * 2,
        out_specs=[anywhere] * 4,
        scratch_shapes=[
            dma((parts, 2, length)),
            dma((parts, length)),
            dma((parts, length)),
            dma((parts, length)),
            dma((parts, n_row)),
            dma((parts, n_row)),
            dma((n_row,)),
            dma((n_row,)),
            dma((2,)),
            dma((2,)),
            dma((2,)),
        ],
        compiler_params=pltpu.CompilerParams(collective_id=0, has_side_effects=True),
        name="gather",
    )(blocks, meta)


def list_products(left_cols, count, per_row, cols, slots, keep, keeps, inverse, sub_rows, found):
    width = inverse.shape[0] // sub_rows

    def clear(at, carry):
        for k in range(8):
            inverse[at * 8 + k] = -1
        return carry

    def mark(at, carry):
        column = keep[at]

        @pl.when(column >= 0)
        def _():
            inverse[at // keeps * width + jnp.maximum(column, 0)] = at

        return carry

    lax.fori_loop(0, inverse.shape[0] // 8, clear, 0)
    lax.fori_loop(0, sub_rows * keeps, mark, 0)
    lefts, rights, results = found

    def one(at, total):
        column = left_cols[at]
        present = column >= 0
        base = jnp.maximum(column, 0) * slots
        line = at // per_row * width
        for a in range(slots):
            result = inverse[line + cols[base + a]]
            lefts[total] = at
            rights[total] = base + a
            results[total] = result
            total = total + jnp.where(present & (result >= 0), 1, 0)
        return total

    return lax.fori_loop(0, count, one, 0)


def multiply(total, load_left, right_hbm, acc, spare, found, buffers, sems):
    lefts, rights, results = found
    for k in range(GROUP):
        lefts[total + k] = 0
        rights[total + k] = 0
        results[total + k] = spare
    groups = (total + GROUP - 1) // GROUP
    ahead = DEPTH // GROUP

    def copies(group, go):
        slot = lax.rem(group, ahead) * GROUP
        for k in range(GROUP):
            copy = pltpu.make_async_copy(
                right_hbm.at[rights[group * GROUP + k]], buffers.at[slot + k], sems.at[slot + k]
            )
            if go:
                copy.start()
            else:
                copy.wait()
        return slot

    def prime(group, carry):
        copies(group, True)
        return carry

    lax.fori_loop(0, jnp.minimum(groups, ahead), prime, 0)

    def step(group, carry):
        slot = copies(group, False)
        products = [
            jnp.dot(
                load_left(lefts[group * GROUP + k]),
                buffers[slot + k],
                preferred_element_type=jnp.float32,
            )
            for k in range(GROUP)
        ]
        for k in range(GROUP):
            acc[results[group * GROUP + k]] += products[k]

        @pl.when(group + ahead < groups)
        def _():
            copies(group + ahead, True)

        return carry

    lax.fori_loop(0, groups, step, 0)


def square_kernel(
    dims, left_cols, cols, keep, left, right, out, half, acc, buffers, l1, l2, l3, inverse, sems
):
    sub_rows, slots, keeps = dims
    count = sub_rows * keeps
    acc[...] = jnp.zeros_like(acc)
    found = (l1, l2, l3)
    total = list_products(
        left_cols, left.shape[0], left.shape[0] // sub_rows, cols, slots, keep, keeps, inverse, sub_rows, found
    )
    multiply(total, lambda at: left[at], right, acc, count, found, buffers, sems)

    def finish(at, carry):
        value = acc[at]
        out[at] = value
        half[at] = value.astype(half.dtype)
        return carry

    lax.fori_loop(0, count, finish, 0)


def cube_kernel(
    dims, left_cols, cols, keep, left, right, base, out, acc, buffers, l1, l2, l3, inverse, sems, *, scale
):
    sub_rows, slots, keeps = dims
    count = sub_rows * keeps
    acc[...] = jnp.zeros_like(acc)
    found = (l1, l2, l3)
    total = list_products(
        left_cols, left.shape[0], left.shape[0] // sub_rows, cols, slots, keep, keeps, inverse, sub_rows, found
    )
    multiply(total, lambda at: left[at], right, acc, count, found, buffers, sems)

    def finish(at, carry):
        out[at] = (scale * base[at] - 2.0 * acc[at]).astype(out.dtype)
        return carry

    lax.fori_loop(0, count, finish, 0)


def products(kernel, outs, dims, left_cols, cols, keep, left, right, extra, width, name):
    sub_rows, slots, keeps = dims
    block = left.shape[1:]
    count = sub_rows * keeps
    entries = left.shape[0] * slots + GROUP
    smem = pl.BlockSpec(memory_space=pltpu.SMEM)
    vmem = pl.BlockSpec(memory_space=pltpu.VMEM)
    hbm = pl.BlockSpec(memory_space=pltpu.HBM)
    scalars = pltpu.SMEM((entries,), jnp.int32)
    return pl.pallas_call(
        functools.partial(kernel, dims),
        out_shape=tuple(jax.ShapeDtypeStruct((count,) + block, t) for t in outs),
        in_specs=[smem] * 3 + [vmem, hbm] + [vmem] * len(extra),
        out_specs=tuple(vmem for _ in outs),
        scratch_shapes=[
            pltpu.VMEM((count + 1,) + block, jnp.float32),
            pltpu.VMEM((DEPTH,) + block, right.dtype),
            scalars,
            scalars,
            scalars,
            pltpu.SMEM((sub_rows * width,), jnp.int32),
            pltpu.SemaphoreType.DMA((DEPTH,)),
        ],
        compiler_params=pltpu.CompilerParams(vmem_limit_bytes=48 * 1024 * 1024),
        cost_estimate=pl.CostEstimate(
            flops=2 * 2 * count * 128**3, bytes_accessed=30_000_000, transcendentals=0
        ),
        name=name,
    )(left_cols, cols, keep, left, right, *extra)


def shards(p_blocks, p_cols, keep_cols):
    n_row = lax.axis_size("row")
    layer = lax.axis_index("layer")
    rows, slots = p_blocks.shape[:2]
    block = p_blocks.shape[2:]
    keeps = keep_cols.shape[1]
    sub_rows = rows // lax.axis_size("layer")
    width = n_row * rows
    dims = (sub_rows, slots, keeps)

    unused = jnp.zeros((rows, LANES - slots - keeps), jnp.int32)
    meta = jnp.concatenate([p_cols, keep_cols, unused], axis=1)
    full, table, other_blocks, other_meta = gather(p_blocks, meta, n_row)

    def own(values):
        return lax.dynamic_slice_in_dim(values, layer * sub_rows, sub_rows, 0)

    right = full.reshape((width * slots,) + block)
    cols = table[:, :, :slots].reshape(-1)
    meta_here, meta_there = own(meta), own(other_meta)
    keep_here = meta_here[:, slots : slots + keeps].reshape(-1)
    keep_there = meta_there[:, slots : slots + keeps].reshape(-1)
    left = jnp.concatenate([own(p_blocks), other_blocks], axis=1).reshape((-1,) + block)
    left_cols = jnp.concatenate([meta_here[:, :slots], meta_there[:, :slots]], axis=1).reshape(-1)

    square, half = products(
        square_kernel,
        (jnp.float32, jnp.bfloat16),
        dims,
        left_cols,
        cols,
        keep_here,
        left,
        right,
        (),
        width,
        "square",
    )
    half_there = lax.ppermute(half, "col", [(0, 1), (1, 0)])
    (partial,) = products(
        functools.partial(cube_kernel, scale=3.0),
        (jnp.float32,),
        dims,
        keep_here,
        cols,
        keep_here,
        half,
        right,
        (square,),
        width,
        "cube_here",
    )
    (result,) = products(
        functools.partial(cube_kernel, scale=1.0),
        (jnp.bfloat16,),
        dims,
        keep_there,
        cols,
        keep_here,
        half_there,
        right,
        (partial,),
        width,
        "cube_there",
    )
    return result.reshape((sub_rows, keeps) + block)


def solution(mesh):
    placed = (P("row", "col", None, None), P("row", "col"), P("row", "col"))
    return jax.shard_map(
        shards,
        mesh=mesh,
        in_specs=placed,
        out_specs=P(("row", "layer"), "col", None, None),
        check_vma=False,
    )
```

```python
import functools

import jax
import jax.numpy as jnp
from jax import lax
from jax.experimental import pallas as pl
from jax.experimental.pallas import tpu as pltpu
from jax.sharding import PartitionSpec as P

MESH = pl.DeviceIdType.MESH
LANES = 128
DEPTH = 16
GROUP = 4


def gather_kernel(
    n_row,
    lines,
    blocks_ref,
    meta_ref,
    full_ref,
    table_ref,
    other_ref,
    other_meta_ref,
    z_send,
    z_recv,
    y_send,
    y_recv,
    c_send,
    c_recv,
    m_send,
    m_recv,
    x_send,
    x_recv,
    local,
):
    row, col, layer = lax.axis_index("row"), lax.axis_index("col"), lax.axis_index("layer")
    length = n_row // 2
    z, y = row // 2, row % 2
    half = blocks_ref.shape[0] // 2
    mine = pl.ds(pl.multiple_of(layer * half, half), half)
    theirs = pl.ds(pl.multiple_of((1 - layer) * half, half), half)
    parts = len(lines)

    barrier = pltpu.get_barrier_semaphore()
    for step in range(1, n_row):
        pl.semaphore_signal(
            barrier, inc=1, device_id=(lax.rem(row + step, n_row), col, layer), device_id_type=MESH
        )
    pl.semaphore_signal(barrier, inc=1, device_id=(row, 1 - col, layer), device_id_type=MESH)
    pl.semaphore_signal(barrier, inc=1, device_id=(row, col, 1 - layer), device_id_type=MESH)
    pl.semaphore_wait(barrier, n_row + 1)

    def source(part, chunk):
        lo, hi = lines[part]
        if chunk is None:
            return blocks_ref.at[mine, pl.ds(lo, hi - lo)]
        return full_ref.at[chunk, mine, pl.ds(lo, hi - lo)]

    def target(part, chunk, rows):
        lo, hi = lines[part]
        return full_ref.at[chunk, rows, pl.ds(lo, hi - lo)]

    def z_copy(part, chunk, way, own):
        return pltpu.make_async_remote_copy(
            src_ref=source(part, None if own else chunk),
            dst_ref=target(part, chunk, mine),
            send_sem=z_send.at[part, way, chunk],
            recv_sem=z_recv.at[part, chunk],
            device_id=(row + (2 if way else -2), col, layer),
            device_id_type=MESH,
        )

    def y_copy(part, pos, own, arriving=False):
        chunk = pos * 2 + (1 - y if arriving else y)
        return pltpu.make_async_remote_copy(
            src_ref=source(part, None if own else chunk),
            dst_ref=target(part, chunk, mine),
            send_sem=y_send.at[part, pos],
            recv_sem=y_recv.at[part, pos],
            device_id=(z * 2 + 1 - y, col, layer),
            device_id_type=MESH,
        )

    def c_copy(part, chunk, arriving=False):
        return pltpu.make_async_remote_copy(
            src_ref=source(part, chunk),
            dst_ref=target(part, chunk, theirs if arriving else mine),
            send_sem=c_send.at[part, chunk],
            recv_sem=c_recv.at[part, chunk],
            device_id=(row, col, 1 - layer),
            device_id_type=MESH,
        )

    def m_copy(step, arriving=False):
        return pltpu.make_async_remote_copy(
            src_ref=meta_ref,
            dst_ref=table_ref.at[lax.rem(row - step + n_row, n_row) if arriving else row],
            send_sem=m_send.at[step],
            recv_sem=m_recv.at[step],
            device_id=(lax.rem(row + step, n_row), col, layer),
            device_id_type=MESH,
        )

    x_block = pltpu.make_async_remote_copy(
        src_ref=blocks_ref.at[mine],
        dst_ref=other_ref,
        send_sem=x_send.at[0],
        recv_sem=x_recv.at[0],
        device_id=(row, 1 - col, layer),
        device_id_type=MESH,
    )
    x_meta = pltpu.make_async_remote_copy(
        src_ref=meta_ref,
        dst_ref=other_meta_ref,
        send_sem=x_send.at[1],
        recv_sem=x_recv.at[1],
        device_id=(row, 1 - col, layer),
        device_id_type=MESH,
    )

    straight = range(parts - 1)
    turned = parts - 1

    def to_sides(part, chunk, own):
        @pl.when(z < length - 1)
        def _():
            z_copy(part, chunk, 1, own).start()

        @pl.when(z > 0)
        def _():
            z_copy(part, chunk, 0, own).start()

    y_copy(turned, z, True).start()
    for part in straight:
        y_copy(part, z, True).start()
        to_sides(part, row, True)
    to_sides(turned, row, True)
    x_block.start()
    x_meta.start()
    for step in range(1, n_row):
        m_copy(step).start()
    own_blocks = pltpu.make_async_copy(blocks_ref, full_ref.at[row], local.at[0])
    own_meta = pltpu.make_async_copy(meta_ref, table_ref.at[row], local.at[1])
    own_blocks.start()
    own_meta.start()

    def from_side(part, pos, way, side, on_to_y):
        chunk = pos * 2 + side
        z_copy(part, chunk, way, False).wait_recv()

        @pl.when((z < length - 1) if way else (z > 0))
        def _():
            z_copy(part, chunk, way, False).start()

        if on_to_y:
            y_copy(part, pos, False).start()
        c_copy(part, chunk).start()

    def from_y(part, pos):
        y_copy(part, pos, False, True).wait_recv()
        c_copy(part, pos * 2 + 1 - y).start()

    def both_sides(step, act):
        @pl.when(z - step >= 0)
        def _():
            act(z - step, 1)

        @pl.when(z + step < length)
        def _():
            act(z + step, 0)

    from_y(turned, z)
    to_sides(turned, z * 2 + 1 - y, False)
    for step in range(1, length + 1):
        if step < length:
            for part in straight:
                both_sides(step, lambda pos, way: from_side(part, pos, way, y, True))
        if step > 1:
            both_sides(step - 1, lambda pos, way: from_side(turned, pos, way, y, False))
            both_sides(step - 1, lambda pos, way: from_side(turned, pos, way, 1 - y, False))
        for part in straight:
            if step == 1:
                from_y(part, z)
            else:
                both_sides(step - 1, lambda pos, way: from_y(part, pos))

    for step in range(1, n_row):
        m_copy(step, True).wait_recv()
        m_copy(step).wait_send()
    x_block.wait()
    x_meta.wait()
    own_blocks.wait()
    own_meta.wait()

    for part in range(parts):
        for pos in range(length):
            if part != turned:
                y_copy(part, pos, False).wait_send()
            for side in range(2):

                @pl.when((pos <= z) & (z < length - 1) & ((part == turned) | (y == side)))
                def _():
                    z_copy(part, pos * 2 + side, 1, False).wait_send()

                @pl.when((pos >= z) & (z > 0) & ((part == turned) | (y == side)))
                def _():
                    z_copy(part, pos * 2 + side, 0, False).wait_send()

        if part == turned:
            y_copy(part, z, False).wait_send()
        for chunk in range(n_row):

            @pl.when(chunk != row)
            def _():
                c_copy(part, chunk).wait_send()
                c_copy(part, chunk, True).wait_recv()


def gather(blocks, meta, n_row):
    rows, slots = blocks.shape[:2]
    turn = slots - max(slots // 5, 1)
    middle = turn // 2
    lines = ((0, middle), (middle, turn), (turn, slots))
    parts = len(lines)
    length = n_row // 2
    anywhere = pl.BlockSpec(memory_space=pl.ANY)
    dma = pltpu.SemaphoreType.DMA
    return pl.pallas_call(
        functools.partial(gather_kernel, n_row, lines),
        out_shape=(
            jax.ShapeDtypeStruct((n_row,) + blocks.shape, blocks.dtype),
            jax.ShapeDtypeStruct((n_row,) + meta.shape, meta.dtype),
            jax.ShapeDtypeStruct((rows // 2,) + blocks.shape[1:], blocks.dtype),
            jax.ShapeDtypeStruct(meta.shape, meta.dtype),
        ),
        in_specs=[anywhere] * 2,
        out_specs=[anywhere] * 4,
        scratch_shapes=[
            dma((parts, 2, n_row)),
            dma((parts, n_row)),
            dma((parts, length)),
            dma((parts, length)),
            dma((parts, n_row)),
            dma((parts, n_row)),
            dma((n_row,)),
            dma((n_row,)),
            dma((2,)),
            dma((2,)),
            dma((2,)),
        ],
        compiler_params=pltpu.CompilerParams(collective_id=0, has_side_effects=True),
        name="gather",
    )(blocks, meta)


def list_products(left_cols, count, per_row, cols, slots, keep, keeps, inverse, sub_rows, found):
    width = inverse.shape[0] // sub_rows

    def clear(at, carry):
        for k in range(8):
            inverse[at * 8 + k] = -1
        return carry

    def mark(at, carry):
        column = keep[at]

        @pl.when(column >= 0)
        def _():
            inverse[at // keeps * width + jnp.maximum(column, 0)] = at

        return carry

    lax.fori_loop(0, inverse.shape[0] // 8, clear, 0)
    lax.fori_loop(0, sub_rows * keeps, mark, 0)
    lefts, rights, results = found

    def one(at, total):
        column = left_cols[at]
        present = column >= 0
        base = jnp.maximum(column, 0) * slots
        line = at // per_row * width
        for a in range(slots):
            result = inverse[line + cols[base + a]]
            lefts[total] = at
            rights[total] = base + a
            results[total] = result
            total = total + jnp.where(present & (result >= 0), 1, 0)
        return total

    return lax.fori_loop(0, count, one, 0)


def multiply(total, load_left, right_hbm, acc, spare, found, buffers, sems):
    lefts, rights, results = found
    for k in range(GROUP):
        lefts[total + k] = 0
        rights[total + k] = 0
        results[total + k] = spare
    groups = (total + GROUP - 1) // GROUP
    ahead = DEPTH // GROUP

    def copies(group, go):
        slot = lax.rem(group, ahead) * GROUP
        for k in range(GROUP):
            copy = pltpu.make_async_copy(
                right_hbm.at[rights[group * GROUP + k]], buffers.at[slot + k], sems.at[slot + k]
            )
            if go:
                copy.start()
            else:
                copy.wait()
        return slot

    def prime(group, carry):
        copies(group, True)
        return carry

    lax.fori_loop(0, jnp.minimum(groups, ahead), prime, 0)

    def step(group, carry):
        slot = copies(group, False)
        products = [
            jnp.dot(
                load_left(lefts[group * GROUP + k]),
                buffers[slot + k],
                preferred_element_type=jnp.float32,
            )
            for k in range(GROUP)
        ]
        for k in range(GROUP):
            acc[results[group * GROUP + k]] += products[k]

        @pl.when(group + ahead < groups)
        def _():
            copies(group + ahead, True)

        return carry

    lax.fori_loop(0, groups, step, 0)


def each_block(count, act):
    def step(at, carry):
        act(at)
        return carry

    lax.fori_loop(0, count, step, 0)


def listed(dims, left_cols, cols, keep, left, found, inverse):
    sub_rows, slots, keeps = dims
    return list_products(
        left_cols, left.shape[0], left.shape[0] // sub_rows, cols, slots, keep, keeps, inverse, sub_rows, found
    )


def square_kernel(
    dims, left_cols, cols, keep, left, right, out, half, acc, buffers, l1, l2, l3, inverse, sems, own_sem
):
    count = dims[0] * dims[2]
    acc[...] = jnp.zeros_like(acc)
    found = (l1, l2, l3)
    total = listed(dims, left_cols, cols, keep, left, found, inverse)
    multiply(total, lambda at: left[at], right, acc, count, found, buffers, sems)
    save = pltpu.make_async_copy(acc.at[pl.ds(0, count)], out, own_sem)
    save.start()

    def finish(at):
        half[at] = acc[at].astype(half.dtype)

    each_block(count, finish)
    save.wait()


def cube_here_kernel(
    dims, left_cols, cols, keep, left, right, base, out, acc, buffers, l1, l2, l3, inverse, sems, own_sem
):
    count = dims[0] * dims[2]
    load = pltpu.make_async_copy(base, acc.at[pl.ds(0, count)], own_sem)
    load.start()
    found = (l1, l2, l3)
    total = listed(dims, left_cols, cols, keep, left, found, inverse)
    load.wait()

    def begin(at):
        acc[at] = -1.5 * acc[at]

    each_block(count, begin)
    multiply(total, lambda at: left[at], right, acc, count, found, buffers, sems)
    save = pltpu.make_async_copy(acc.at[pl.ds(0, count)], out, own_sem)
    save.start()
    save.wait()


def cube_there_kernel(
    dims, first, left_cols, cols, keep, left, right, base, *rest
):
    out, acc, buffers, l1, l2, l3, inverse, sems, own_sem, done = rest[-10:]
    count = dims[0] * dims[2]
    load = pltpu.make_async_copy(base, acc.at[pl.ds(0, count)], own_sem)
    load.start()
    found = (l1, l2, l3)
    total = listed(dims, left_cols, cols, keep, left, found, inverse)
    load.wait()
    multiply(total, lambda at: left[at], right, acc, count, found, buffers, sems)

    def finish(at):
        done[at] = (-2.0 * acc[at]).astype(done.dtype)

    each_block(count, finish)
    save = pltpu.make_async_copy(done, out.at[pl.ds(first, count)], own_sem)
    save.start()
    save.wait()


def products(kernel, outs, dims, left_cols, cols, keep, left, right, extra, width, name, more=(), alias=None):
    sub_rows, slots, keeps = dims
    block = left.shape[1:]
    count = sub_rows * keeps
    entries = left.shape[0] * slots + GROUP
    smem = pl.BlockSpec(memory_space=pltpu.SMEM)
    vmem = pl.BlockSpec(memory_space=pltpu.VMEM)
    hbm = pl.BlockSpec(memory_space=pltpu.HBM)
    scalars = pltpu.SMEM((entries,), jnp.int32)
    return pl.pallas_call(
        kernel,
        out_shape=tuple(jax.ShapeDtypeStruct((n,) + block, t) for n, t, place in outs),
        in_specs=[smem] * 3 + [vmem, hbm] + [hbm] * len(extra),
        out_specs=tuple({"vmem": vmem, "hbm": hbm}[place] for n, t, place in outs),
        scratch_shapes=[
            pltpu.VMEM((count + 1,) + block, jnp.float32),
            pltpu.VMEM((DEPTH,) + block, right.dtype),
            scalars,
            scalars,
            scalars,
            pltpu.SMEM((sub_rows * width,), jnp.int32),
            pltpu.SemaphoreType.DMA((DEPTH,)),
            pltpu.SemaphoreType.DMA,
            *more,
        ],
        input_output_aliases={} if alias is None else {alias: 0},
        compiler_params=pltpu.CompilerParams(vmem_limit_bytes=48 * 1024 * 1024),
        cost_estimate=pl.CostEstimate(
            flops=2 * 2 * count * 128**3, bytes_accessed=15_000_000, transcendentals=0
        ),
        name=name,
    )(left_cols, cols, keep, left, right, *extra)


def shards(p_blocks, p_cols, keep_cols):
    n_row = lax.axis_size("row")
    layer = lax.axis_index("layer")
    rows, slots = p_blocks.shape[:2]
    block = p_blocks.shape[2:]
    keeps = keep_cols.shape[1]
    sub_rows = rows // lax.axis_size("layer")
    width = n_row * rows

    unused = jnp.zeros((rows, LANES - slots - keeps), jnp.int32)
    meta = jnp.concatenate([p_cols, keep_cols, unused], axis=1)
    full, table, other_blocks, other_meta = gather(p_blocks, meta, n_row)

    def own(values):
        return lax.dynamic_slice_in_dim(values, layer * sub_rows, sub_rows, 0)

    right = full.reshape((width * slots,) + block)
    cols = table[:, :, :slots].reshape(-1)
    meta_here, meta_there = own(meta), own(other_meta)
    blocks_here = own(p_blocks)
    lots = 2 if sub_rows % 2 == 0 else 1
    lot = sub_rows // lots
    dims = (lot, slots, keeps)
    count = lot * keeps
    f32, bf16 = jnp.float32, jnp.bfloat16
    state = []
    for at in range(lots):
        here = meta_here[at * lot : (at + 1) * lot]
        there = meta_there[at * lot : (at + 1) * lot]
        keep_here = here[:, slots : slots + keeps].reshape(-1)
        keep_there = there[:, slots : slots + keeps].reshape(-1)
        left = jnp.concatenate(
            [blocks_here[at * lot : (at + 1) * lot], other_blocks[at * lot : (at + 1) * lot]], axis=1
        ).reshape((-1,) + block)
        left_cols = jnp.concatenate([here[:, :slots], there[:, :slots]], axis=1).reshape(-1)
        square, half = products(
            functools.partial(square_kernel, dims),
            ((count, f32, "hbm"), (count, bf16, "vmem")),
            dims,
            left_cols,
            cols,
            keep_here,
            left,
            right,
            (),
            width,
            f"square_{at}",
        )
        half_there = lax.ppermute(half, "col", [(0, 1), (1, 0)])
        state.append((keep_here, keep_there, square, half, half_there))
    partials = []
    for at, (keep_here, keep_there, square, half, half_there) in enumerate(state):
        (partial,) = products(
            functools.partial(cube_here_kernel, dims),
            ((count, f32, "hbm"),),
            dims,
            keep_here,
            cols,
            keep_here,
            half,
            right,
            (square,),
            width,
            f"cube_here_{at}",
        )
        partials.append(partial)
    result = None
    for at, (keep_here, keep_there, square, half, half_there) in enumerate(state):
        (result,) = products(
            functools.partial(cube_there_kernel, dims, at * count),
            ((lots * count, bf16, "hbm"),),
            dims,
            keep_there,
            cols,
            keep_here,
            half_there,
            right,
            (partials[at],) + (() if at == 0 else (result,)),
            width,
            f"cube_there_{at}",
            (pltpu.VMEM((count,) + block, bf16),),
            None if at == 0 else 6,
        )
    return result.reshape((sub_rows, keeps) + block)


def solution(mesh):
    placed = (P("row", "col", None, None), P("row", "col"), P("row", "col"))
    return jax.shard_map(
        shards,
        mesh=mesh,
        in_specs=placed,
        out_specs=P(("row", "layer"), "col", None, None),
        check_vma=False,
    )
```

```python
import functools

import jax
import jax.numpy as jnp
from jax import lax
from jax.experimental import pallas as pl
from jax.experimental.pallas import tpu as pltpu
from jax.sharding import PartitionSpec as P

MESH = pl.DeviceIdType.MESH
LANES = 128
DEPTH = 16
GROUP = 4


def gather_kernel(
    n_row,
    lines,
    blocks_ref,
    meta_ref,
    full_ref,
    table_ref,
    other_ref,
    other_meta_ref,
    z_send,
    z_recv,
    y_send,
    y_recv,
    c_send,
    c_recv,
    m_send,
    m_recv,
    x_send,
    x_recv,
    local,
):
    row, col, layer = lax.axis_index("row"), lax.axis_index("col"), lax.axis_index("layer")
    length = n_row // 2
    z, y = row // 2, row % 2
    half = blocks_ref.shape[0] // 2
    mine = pl.ds(pl.multiple_of(layer * half, half), half)
    theirs = pl.ds(pl.multiple_of((1 - layer) * half, half), half)
    parts = len(lines)

    barrier = pltpu.get_barrier_semaphore()
    for step in range(1, n_row):
        pl.semaphore_signal(
            barrier, inc=1, device_id=(lax.rem(row + step, n_row), col, layer), device_id_type=MESH
        )
    pl.semaphore_signal(barrier, inc=1, device_id=(row, 1 - col, layer), device_id_type=MESH)
    pl.semaphore_signal(barrier, inc=1, device_id=(row, col, 1 - layer), device_id_type=MESH)
    pl.semaphore_wait(barrier, n_row + 1)

    def source(part, chunk):
        lo, hi = lines[part]
        if chunk is None:
            return blocks_ref.at[mine, pl.ds(lo, hi - lo)]
        return full_ref.at[chunk, mine, pl.ds(lo, hi - lo)]

    def target(part, chunk, rows):
        lo, hi = lines[part]
        return full_ref.at[chunk, rows, pl.ds(lo, hi - lo)]

    def z_copy(part, chunk, way, own):
        return pltpu.make_async_remote_copy(
            src_ref=source(part, None if own else chunk),
            dst_ref=target(part, chunk, mine),
            send_sem=z_send.at[part, way, chunk],
            recv_sem=z_recv.at[part, chunk],
            device_id=(row + (2 if way else -2), col, layer),
            device_id_type=MESH,
        )

    def y_copy(part, pos, own, arriving=False):
        chunk = pos * 2 + (1 - y if arriving else y)
        return pltpu.make_async_remote_copy(
            src_ref=source(part, None if own else chunk),
            dst_ref=target(part, chunk, mine),
            send_sem=y_send.at[part, pos],
            recv_sem=y_recv.at[part, pos],
            device_id=(z * 2 + 1 - y, col, layer),
            device_id_type=MESH,
        )

    def c_copy(part, chunk, arriving=False):
        return pltpu.make_async_remote_copy(
            src_ref=source(part, chunk),
            dst_ref=target(part, chunk, theirs if arriving else mine),
            send_sem=c_send.at[part, chunk],
            recv_sem=c_recv.at[part, chunk],
            device_id=(row, col, 1 - layer),
            device_id_type=MESH,
        )

    def m_copy(step, arriving=False):
        return pltpu.make_async_remote_copy(
            src_ref=meta_ref,
            dst_ref=table_ref.at[lax.rem(row - step + n_row, n_row) if arriving else row],
            send_sem=m_send.at[step],
            recv_sem=m_recv.at[step],
            device_id=(lax.rem(row + step, n_row), col, layer),
            device_id_type=MESH,
        )

    x_block = pltpu.make_async_remote_copy(
        src_ref=blocks_ref.at[mine],
        dst_ref=other_ref,
        send_sem=x_send.at[0],
        recv_sem=x_recv.at[0],
        device_id=(row, 1 - col, layer),
        device_id_type=MESH,
    )
    x_meta = pltpu.make_async_remote_copy(
        src_ref=meta_ref,
        dst_ref=other_meta_ref,
        send_sem=x_send.at[1],
        recv_sem=x_recv.at[1],
        device_id=(row, 1 - col, layer),
        device_id_type=MESH,
    )

    straight = range(parts - 1)
    turned = parts - 1

    def to_sides(part, chunk, own):
        @pl.when(z < length - 1)
        def _():
            z_copy(part, chunk, 1, own).start()

        @pl.when(z > 0)
        def _():
            z_copy(part, chunk, 0, own).start()

    y_copy(turned, z, True).start()
    for part in straight:
        y_copy(part, z, True).start()
        to_sides(part, row, True)
    to_sides(turned, row, True)
    x_block.start()
    x_meta.start()
    for step in range(1, n_row):
        m_copy(step).start()
    own_blocks = pltpu.make_async_copy(blocks_ref, full_ref.at[row], local.at[0])
    own_meta = pltpu.make_async_copy(meta_ref, table_ref.at[row], local.at[1])
    own_blocks.start()
    own_meta.start()

    def from_side(part, pos, way, side, on_to_y):
        chunk = pos * 2 + side
        z_copy(part, chunk, way, False).wait_recv()

        @pl.when((z < length - 1) if way else (z > 0))
        def _():
            z_copy(part, chunk, way, False).start()

        if on_to_y:
            y_copy(part, pos, False).start()
        c_copy(part, chunk).start()

    def from_y(part, pos):
        y_copy(part, pos, False, True).wait_recv()
        c_copy(part, pos * 2 + 1 - y).start()

    def both_sides(step, act):
        @pl.when(z - step >= 0)
        def _():
            act(z - step, 1)

        @pl.when(z + step < length)
        def _():
            act(z + step, 0)

    from_y(turned, z)
    to_sides(turned, z * 2 + 1 - y, False)
    for step in range(1, length + 1):
        if step < length:
            for part in straight:
                both_sides(step, lambda pos, way: from_side(part, pos, way, y, True))
        if step > 1:
            both_sides(step - 1, lambda pos, way: from_side(turned, pos, way, y, False))
            both_sides(step - 1, lambda pos, way: from_side(turned, pos, way, 1 - y, False))
        for part in straight:
            if step == 1:
                from_y(part, z)
            else:
                both_sides(step - 1, lambda pos, way: from_y(part, pos))

    for step in range(1, n_row):
        m_copy(step, True).wait_recv()
        m_copy(step).wait_send()
    x_block.wait()
    x_meta.wait()
    own_blocks.wait()
    own_meta.wait()

    for part in range(parts):
        for pos in range(length):
            if part != turned:
                y_copy(part, pos, False).wait_send()
            for side in range(2):

                @pl.when((pos <= z) & (z < length - 1) & ((part == turned) | (y == side)))
                def _():
                    z_copy(part, pos * 2 + side, 1, False).wait_send()

                @pl.when((pos >= z) & (z > 0) & ((part == turned) | (y == side)))
                def _():
                    z_copy(part, pos * 2 + side, 0, False).wait_send()

        if part == turned:
            y_copy(part, z, False).wait_send()
        for chunk in range(n_row):

            @pl.when(chunk != row)
            def _():
                c_copy(part, chunk).wait_send()
                c_copy(part, chunk, True).wait_recv()


def gather(blocks, meta, n_row):
    rows, slots = blocks.shape[:2]
    lines = tuple((at, at + 1) for at in range(slots))
    parts = len(lines)
    length = n_row // 2
    anywhere = pl.BlockSpec(memory_space=pl.ANY)
    dma = pltpu.SemaphoreType.DMA
    return pl.pallas_call(
        functools.partial(gather_kernel, n_row, lines),
        out_shape=(
            jax.ShapeDtypeStruct((n_row,) + blocks.shape, blocks.dtype),
            jax.ShapeDtypeStruct((n_row,) + meta.shape, meta.dtype),
            jax.ShapeDtypeStruct((rows // 2,) + blocks.shape[1:], blocks.dtype),
            jax.ShapeDtypeStruct(meta.shape, meta.dtype),
        ),
        in_specs=[anywhere] * 2,
        out_specs=[anywhere] * 4,
        scratch_shapes=[
            dma((parts, 2, n_row)),
            dma((parts, n_row)),
            dma((parts, length)),
            dma((parts, length)),
            dma((parts, n_row)),
            dma((parts, n_row)),
            dma((n_row,)),
            dma((n_row,)),
            dma((2,)),
            dma((2,)),
            dma((2,)),
        ],
        compiler_params=pltpu.CompilerParams(collective_id=0, has_side_effects=True),
        name="gather",
    )(blocks, meta)


def list_products(left_cols, count, per_row, cols, slots, keep, keeps, inverse, sub_rows, found):
    width = inverse.shape[0] // sub_rows

    def clear(at, carry):
        for k in range(8):
            inverse[at * 8 + k] = -1
        return carry

    def mark(at, carry):
        column = keep[at]

        @pl.when(column >= 0)
        def _():
            inverse[at // keeps * width + jnp.maximum(column, 0)] = at

        return carry

    lax.fori_loop(0, inverse.shape[0] // 8, clear, 0)
    lax.fori_loop(0, sub_rows * keeps, mark, 0)
    lefts, rights, results = found

    def one(at, total):
        column = left_cols[at]
        present = column >= 0
        base = jnp.maximum(column, 0) * slots
        line = at // per_row * width
        for a in range(slots):
            result = inverse[line + cols[base + a]]
            lefts[total] = at
            rights[total] = base + a
            results[total] = result
            total = total + jnp.where(present & (result >= 0), 1, 0)
        return total

    return lax.fori_loop(0, count, one, 0)


def multiply(total, load_left, right_hbm, acc, spare, found, buffers, sems):
    lefts, rights, results = found
    for k in range(GROUP):
        lefts[total + k] = 0
        rights[total + k] = 0
        results[total + k] = spare
    groups = (total + GROUP - 1) // GROUP
    ahead = DEPTH // GROUP

    def copies(group, go):
        slot = lax.rem(group, ahead) * GROUP
        for k in range(GROUP):
            copy = pltpu.make_async_copy(
                right_hbm.at[rights[group * GROUP + k]], buffers.at[slot + k], sems.at[slot + k]
            )
            if go:
                copy.start()
            else:
                copy.wait()
        return slot

    def prime(group, carry):
        copies(group, True)
        return carry

    lax.fori_loop(0, jnp.minimum(groups, ahead), prime, 0)

    def step(group, carry):
        slot = copies(group, False)
        products = [
            jnp.dot(
                load_left(lefts[group * GROUP + k]),
                buffers[slot + k],
                preferred_element_type=jnp.float32,
            )
            for k in range(GROUP)
        ]
        for k in range(GROUP):
            acc[results[group * GROUP + k]] += products[k]

        @pl.when(group + ahead < groups)
        def _():
            copies(group + ahead, True)

        return carry

    lax.fori_loop(0, groups, step, 0)


def each_block(count, act):
    def step(at, carry):
        act(at)
        return carry

    lax.fori_loop(0, count, step, 0)


def listed(dims, left_cols, cols, keep, left, found, inverse):
    sub_rows, slots, keeps = dims
    return list_products(
        left_cols, left.shape[0], left.shape[0] // sub_rows, cols, slots, keep, keeps, inverse, sub_rows, found
    )


def square_kernel(
    dims, first, left_cols, cols, keep, here, there, right, *rest
):
    out, half, acc, buffers, l1, l2, l3, inverse, sems, own_sem, left, rounded, left_sems, half_sem = rest[-14:]
    sub_rows, slots, keeps = dims
    count = sub_rows * keeps
    layer = lax.axis_index("layer")
    start = layer * there.shape[0] + first
    loads = []
    for row in range(sub_rows):
        for at, blocks in enumerate((here.at[start + row], there.at[first + row])):
            loads.append(
                pltpu.make_async_copy(
                    blocks, left.at[pl.ds((2 * row + at) * slots, slots)], left_sems.at[2 * row + at]
                )
            )
    for load in loads:
        load.start()
    acc[...] = jnp.zeros_like(acc)
    found = (l1, l2, l3)
    total = listed(dims, left_cols, cols, keep, left, found, inverse)
    for load in loads:
        load.wait()
    multiply(total, lambda at: left[at], right, acc, count, found, buffers, sems)
    save = pltpu.make_async_copy(acc.at[pl.ds(0, count)], out, own_sem)
    save.start()

    def finish(at):
        rounded[at] = acc[at].astype(rounded.dtype)

    each_block(count, finish)
    send = pltpu.make_async_copy(rounded, half, half_sem)
    send.start()
    send.wait()
    save.wait()


def cube_here_kernel(
    dims, left_cols, cols, keep, left, right, base, out, acc, buffers, l1, l2, l3, inverse, sems, own_sem
):
    count = dims[0] * dims[2]
    load = pltpu.make_async_copy(base, acc.at[pl.ds(0, count)], own_sem)
    load.start()
    found = (l1, l2, l3)
    total = listed(dims, left_cols, cols, keep, left, found, inverse)
    load.wait()

    def begin(at):
        acc[at] = -1.5 * acc[at]

    each_block(count, begin)
    multiply(total, lambda at: left[at], right, acc, count, found, buffers, sems)
    save = pltpu.make_async_copy(acc.at[pl.ds(0, count)], out, own_sem)
    save.start()
    save.wait()


def cube_there_kernel(
    dims, first, left_cols, cols, keep, left, right, base, *rest
):
    out, acc, buffers, l1, l2, l3, inverse, sems, own_sem, done = rest[-10:]
    count = dims[0] * dims[2]
    load = pltpu.make_async_copy(base, acc.at[pl.ds(0, count)], own_sem)
    load.start()
    found = (l1, l2, l3)
    total = listed(dims, left_cols, cols, keep, left, found, inverse)
    load.wait()
    multiply(total, lambda at: left[at], right, acc, count, found, buffers, sems)

    def finish(at):
        done[at] = (-2.0 * acc[at]).astype(done.dtype)

    each_block(count, finish)
    save = pltpu.make_async_copy(done, out.at[pl.ds(first, count)], own_sem)
    save.start()
    save.wait()


def products(kernel, outs, dims, left_cols, cols, keep, left, right, extra, width, name, more=(), alias=None):
    sub_rows, slots, keeps = dims
    block = right.shape[1:]
    count = sub_rows * keeps
    entries = left_cols.shape[0] * slots + GROUP
    smem = pl.BlockSpec(memory_space=pltpu.SMEM)
    vmem = pl.BlockSpec(memory_space=pltpu.VMEM)
    hbm = pl.BlockSpec(memory_space=pltpu.HBM)
    scalars = pltpu.SMEM((entries,), jnp.int32)
    return pl.pallas_call(
        kernel,
        out_shape=tuple(jax.ShapeDtypeStruct((n,) + block, t) for n, t, place in outs),
        in_specs=[smem] * 3 + [vmem if len(left) == 1 else hbm] * len(left) + [hbm] * (1 + len(extra)),
        out_specs=tuple({"vmem": vmem, "hbm": hbm}[place] for n, t, place in outs),
        scratch_shapes=[
            pltpu.VMEM((count + 1,) + block, jnp.float32),
            pltpu.VMEM((DEPTH,) + block, right.dtype),
            scalars,
            scalars,
            scalars,
            pltpu.SMEM((sub_rows * width,), jnp.int32),
            pltpu.SemaphoreType.DMA((DEPTH,)),
            pltpu.SemaphoreType.DMA,
            *more,
        ],
        input_output_aliases={} if alias is None else {alias: 0},
        compiler_params=pltpu.CompilerParams(vmem_limit_bytes=48 * 1024 * 1024),
        cost_estimate=pl.CostEstimate(
            flops=2 * 2 * count * 128**3, bytes_accessed=15_000_000, transcendentals=0
        ),
        name=name,
    )(left_cols, cols, keep, *left, right, *extra)


def shards(p_blocks, p_cols, keep_cols):
    n_row = lax.axis_size("row")
    layer = lax.axis_index("layer")
    rows, slots = p_blocks.shape[:2]
    block = p_blocks.shape[2:]
    keeps = keep_cols.shape[1]
    sub_rows = rows // lax.axis_size("layer")
    width = n_row * rows

    unused = jnp.zeros((rows, LANES - slots - keeps), jnp.int32)
    meta = jnp.concatenate([p_cols, keep_cols, unused], axis=1)
    full, table, other_blocks, other_meta = gather(p_blocks, meta, n_row)

    def own(values):
        return lax.dynamic_slice_in_dim(values, layer * sub_rows, sub_rows, 0)

    right = full.reshape((width * slots,) + block)
    cols = table[:, :, :slots].reshape(-1)
    meta_here, meta_there = own(meta), own(other_meta)
    tail = max(sub_rows // 8, 1)
    middle = (sub_rows - 2 * tail) // 2
    cuts = (0, tail, tail + middle, sub_rows - tail, sub_rows)
    lots = [(lo, hi) for lo, hi in zip(cuts[:-1], cuts[1:]) if hi > lo]
    f32, bf16 = jnp.float32, jnp.bfloat16
    state = []
    for lo, hi in lots:
        dims = (hi - lo, slots, keeps)
        count = (hi - lo) * keeps
        here, there = meta_here[lo:hi], meta_there[lo:hi]
        keep_here = here[:, slots : slots + keeps].reshape(-1)
        keep_there = there[:, slots : slots + keeps].reshape(-1)
        left_cols = jnp.concatenate([here[:, :slots], there[:, :slots]], axis=1).reshape(-1)
        square, half = products(
            functools.partial(square_kernel, dims, lo),
            ((count, f32, "hbm"), (count, bf16, "hbm")),
            dims,
            left_cols,
            cols,
            keep_here,
            (p_blocks, other_blocks),
            right,
            tuple(entry[4] for entry in state[-1:]),
            width,
            f"square_{lo}",
            (
                pltpu.VMEM(((hi - lo) * 2 * slots,) + block, bf16),
                pltpu.VMEM((count,) + block, bf16),
                pltpu.SemaphoreType.DMA(((hi - lo) * 2,)),
                pltpu.SemaphoreType.DMA,
            ),
        )
        half_there = lax.ppermute(half, "col", [(0, 1), (1, 0)])
        state.append((lo, dims, keep_here, keep_there, square, half, half_there))
    partials = []
    for lo, dims, keep_here, keep_there, square, half, half_there in state:
        (partial,) = products(
            functools.partial(cube_here_kernel, dims),
            ((half.shape[0], f32, "hbm"),),
            dims,
            keep_here,
            cols,
            keep_here,
            (half,),
            right,
            (square,),
            width,
            f"cube_here_{lo}",
        )
        partials.append(partial)
    result = None
    for partial, (lo, dims, keep_here, keep_there, square, half, half_there) in zip(partials, state):
        (result,) = products(
            functools.partial(cube_there_kernel, dims, lo * keeps),
            ((sub_rows * keeps, bf16, "hbm"),),
            dims,
            keep_there,
            cols,
            keep_here,
            (half_there,),
            right,
            (partial,) + (() if result is None else (result,)),
            width,
            f"cube_there_{lo}",
            (pltpu.VMEM(half.shape, bf16),),
            None if result is None else 6,
        )
    return result.reshape((sub_rows, keeps) + block)


def solution(mesh):
    placed = (P("row", "col", None, None), P("row", "col"), P("row", "col"))
    return jax.shard_map(
        shards,
        mesh=mesh,
        in_specs=placed,
        out_specs=P(("row", "layer"), "col", None, None),
        check_vma=False,
    )
```

```python
import functools

import jax
import jax.numpy as jnp
from jax import lax
from jax.experimental import pallas as pl
from jax.experimental.pallas import tpu as pltpu
from jax.sharding import PartitionSpec as P

MESH = pl.DeviceIdType.MESH
LANES = 128
DEPTH = 16
GROUP = 4


def gather_kernel(
    n_row,
    lines,
    blocks_ref,
    meta_ref,
    full_ref,
    table_ref,
    other_ref,
    other_meta_ref,
    z_send,
    z_recv,
    y_send,
    y_recv,
    c_send,
    c_recv,
    m_send,
    m_recv,
    x_send,
    x_recv,
    local,
):
    row, col, layer = lax.axis_index("row"), lax.axis_index("col"), lax.axis_index("layer")
    length = n_row // 2
    z, y = row // 2, row % 2
    half = blocks_ref.shape[0] // 2
    mine = pl.ds(pl.multiple_of(layer * half, half), half)
    theirs = pl.ds(pl.multiple_of((1 - layer) * half, half), half)
    parts = len(lines)

    barrier = pltpu.get_barrier_semaphore()
    for step in range(1, n_row):
        pl.semaphore_signal(
            barrier, inc=1, device_id=(lax.rem(row + step, n_row), col, layer), device_id_type=MESH
        )
    pl.semaphore_signal(barrier, inc=1, device_id=(row, 1 - col, layer), device_id_type=MESH)
    pl.semaphore_signal(barrier, inc=1, device_id=(row, col, 1 - layer), device_id_type=MESH)
    pl.semaphore_wait(barrier, n_row + 1)

    def source(part, chunk):
        lo, hi = lines[part]
        if chunk is None:
            return blocks_ref.at[mine, pl.ds(lo, hi - lo)]
        return full_ref.at[chunk, mine, pl.ds(lo, hi - lo)]

    def target(part, chunk, rows):
        lo, hi = lines[part]
        return full_ref.at[chunk, rows, pl.ds(lo, hi - lo)]

    def z_copy(part, chunk, way, own):
        return pltpu.make_async_remote_copy(
            src_ref=source(part, None if own else chunk),
            dst_ref=target(part, chunk, mine),
            send_sem=z_send.at[part, way, chunk],
            recv_sem=z_recv.at[part, chunk],
            device_id=(row + (2 if way else -2), col, layer),
            device_id_type=MESH,
        )

    def y_copy(part, pos, own, arriving=False):
        chunk = pos * 2 + (1 - y if arriving else y)
        return pltpu.make_async_remote_copy(
            src_ref=source(part, None if own else chunk),
            dst_ref=target(part, chunk, mine),
            send_sem=y_send.at[part, pos],
            recv_sem=y_recv.at[part, pos],
            device_id=(z * 2 + 1 - y, col, layer),
            device_id_type=MESH,
        )

    def c_copy(part, chunk, arriving=False):
        return pltpu.make_async_remote_copy(
            src_ref=source(part, chunk),
            dst_ref=target(part, chunk, theirs if arriving else mine),
            send_sem=c_send.at[part, chunk],
            recv_sem=c_recv.at[part, chunk],
            device_id=(row, col, 1 - layer),
            device_id_type=MESH,
        )

    def m_copy(step, arriving=False):
        return pltpu.make_async_remote_copy(
            src_ref=meta_ref,
            dst_ref=table_ref.at[lax.rem(row - step + n_row, n_row) if arriving else row],
            send_sem=m_send.at[step],
            recv_sem=m_recv.at[step],
            device_id=(lax.rem(row + step, n_row), col, layer),
            device_id_type=MESH,
        )

    x_block = pltpu.make_async_remote_copy(
        src_ref=blocks_ref.at[mine],
        dst_ref=other_ref,
        send_sem=x_send.at[0],
        recv_sem=x_recv.at[0],
        device_id=(row, 1 - col, layer),
        device_id_type=MESH,
    )
    x_meta = pltpu.make_async_remote_copy(
        src_ref=meta_ref,
        dst_ref=other_meta_ref,
        send_sem=x_send.at[1],
        recv_sem=x_recv.at[1],
        device_id=(row, 1 - col, layer),
        device_id_type=MESH,
    )

    straight = range(parts - 1)
    turned = parts - 1

    def to_sides(part, chunk, own):
        @pl.when(z < length - 1)
        def _():
            z_copy(part, chunk, 1, own).start()

        @pl.when(z > 0)
        def _():
            z_copy(part, chunk, 0, own).start()

    y_copy(turned, z, True).start()
    for part in straight:
        y_copy(part, z, True).start()
        to_sides(part, row, True)
    to_sides(turned, row, True)
    x_block.start()
    x_meta.start()
    for step in range(1, n_row):
        m_copy(step).start()
    own_blocks = pltpu.make_async_copy(blocks_ref, full_ref.at[row], local.at[0])
    own_meta = pltpu.make_async_copy(meta_ref, table_ref.at[row], local.at[1])
    own_blocks.start()
    own_meta.start()

    def from_side(part, pos, way, side, on_to_y):
        chunk = pos * 2 + side
        z_copy(part, chunk, way, False).wait_recv()

        @pl.when((z < length - 1) if way else (z > 0))
        def _():
            z_copy(part, chunk, way, False).start()

        if on_to_y:
            y_copy(part, pos, False).start()
        c_copy(part, chunk).start()

    def from_y(part, pos):
        y_copy(part, pos, False, True).wait_recv()
        c_copy(part, pos * 2 + 1 - y).start()

    def both_sides(step, act):
        @pl.when(z - step >= 0)
        def _():
            act(z - step, 1)

        @pl.when(z + step < length)
        def _():
            act(z + step, 0)

    from_y(turned, z)
    to_sides(turned, z * 2 + 1 - y, False)
    for step in range(1, length + 1):
        if step < length:
            for part in straight:
                both_sides(step, lambda pos, way: from_side(part, pos, way, y, True))
        if step > 1:
            both_sides(step - 1, lambda pos, way: from_side(turned, pos, way, y, False))
            both_sides(step - 1, lambda pos, way: from_side(turned, pos, way, 1 - y, False))
        for part in straight:
            if step == 1:
                from_y(part, z)
            else:
                both_sides(step - 1, lambda pos, way: from_y(part, pos))

    for step in range(1, n_row):
        m_copy(step, True).wait_recv()
        m_copy(step).wait_send()
    x_block.wait()
    x_meta.wait()
    own_blocks.wait()
    own_meta.wait()

    for part in range(parts):
        for pos in range(length):
            if part != turned:
                y_copy(part, pos, False).wait_send()
            for side in range(2):

                @pl.when((pos <= z) & (z < length - 1) & ((part == turned) | (y == side)))
                def _():
                    z_copy(part, pos * 2 + side, 1, False).wait_send()

                @pl.when((pos >= z) & (z > 0) & ((part == turned) | (y == side)))
                def _():
                    z_copy(part, pos * 2 + side, 0, False).wait_send()

        if part == turned:
            y_copy(part, z, False).wait_send()
        for chunk in range(n_row):

            @pl.when(chunk != row)
            def _():
                c_copy(part, chunk).wait_send()
                c_copy(part, chunk, True).wait_recv()


def gather(blocks, meta, n_row):
    rows, slots = blocks.shape[:2]
    turn = slots - max(slots // 5, 1)
    middle = turn // 2
    lines = ((0, middle), (middle, turn), (turn, slots))
    parts = len(lines)
    length = n_row // 2
    anywhere = pl.BlockSpec(memory_space=pl.ANY)
    dma = pltpu.SemaphoreType.DMA
    return pl.pallas_call(
        functools.partial(gather_kernel, n_row, lines),
        out_shape=(
            jax.ShapeDtypeStruct((n_row,) + blocks.shape, blocks.dtype),
            jax.ShapeDtypeStruct((n_row,) + meta.shape, meta.dtype),
            jax.ShapeDtypeStruct((rows // 2,) + blocks.shape[1:], blocks.dtype),
            jax.ShapeDtypeStruct(meta.shape, meta.dtype),
        ),
        in_specs=[anywhere] * 2,
        out_specs=[anywhere] * 4,
        scratch_shapes=[
            dma((parts, 2, n_row)),
            dma((parts, n_row)),
            dma((parts, length)),
            dma((parts, length)),
            dma((parts, n_row)),
            dma((parts, n_row)),
            dma((n_row,)),
            dma((n_row,)),
            dma((2,)),
            dma((2,)),
            dma((2,)),
        ],
        compiler_params=pltpu.CompilerParams(collective_id=0, has_side_effects=True),
        name="gather",
    )(blocks, meta)


def list_products(left_cols, count, per_row, cols, slots, keep, keeps, inverse, sub_rows, found):
    width = inverse.shape[0] // sub_rows

    def clear(at, carry):
        for k in range(8):
            inverse[at * 8 + k] = -1
        return carry

    def mark(at, carry):
        column = keep[at]

        @pl.when(column >= 0)
        def _():
            inverse[at // keeps * width + jnp.maximum(column, 0)] = at

        return carry

    lax.fori_loop(0, inverse.shape[0] // 8, clear, 0)
    lax.fori_loop(0, sub_rows * keeps, mark, 0)
    lefts, rights, results = found

    def one(at, total):
        column = left_cols[at]
        present = column >= 0
        base = jnp.maximum(column, 0) * slots
        line = at // per_row * width
        for a in range(slots):
            result = inverse[line + cols[base + a]]
            lefts[total] = at
            rights[total] = base + a
            results[total] = result
            total = total + jnp.where(present & (result >= 0), 1, 0)
        return total

    return lax.fori_loop(0, count, one, 0)


def multiply(total, load_left, right_hbm, acc, spare, found, buffers, sems):
    lefts, rights, results = found
    for k in range(GROUP):
        lefts[total + k] = 0
        rights[total + k] = 0
        results[total + k] = spare
    groups = (total + GROUP - 1) // GROUP
    ahead = DEPTH // GROUP

    def copies(group, go):
        slot = lax.rem(group, ahead) * GROUP
        for k in range(GROUP):
            copy = pltpu.make_async_copy(
                right_hbm.at[rights[group * GROUP + k]], buffers.at[slot + k], sems.at[slot + k]
            )
            if go:
                copy.start()
            else:
                copy.wait()
        return slot

    def prime(group, carry):
        copies(group, True)
        return carry

    lax.fori_loop(0, jnp.minimum(groups, ahead), prime, 0)

    def step(group, carry):
        slot = copies(group, False)
        products = [
            jnp.dot(
                load_left(lefts[group * GROUP + k]),
                buffers[slot + k],
                preferred_element_type=jnp.float32,
            )
            for k in range(GROUP)
        ]
        for k in range(GROUP):
            acc[results[group * GROUP + k]] += products[k]

        @pl.when(group + ahead < groups)
        def _():
            copies(group + ahead, True)

        return carry

    lax.fori_loop(0, groups, step, 0)


def each_block(count, act):
    def step(at, carry):
        act(at)
        return carry

    lax.fori_loop(0, count, step, 0)


def listed(dims, left_cols, cols, keep, left, found, inverse):
    sub_rows, slots, keeps = dims
    return list_products(
        left_cols, left.shape[0], left.shape[0] // sub_rows, cols, slots, keep, keeps, inverse, sub_rows, found
    )


def square_kernel(
    dims, first, left_cols, cols, keep, here, there, right, *rest
):
    out, half, acc, buffers, l1, l2, l3, inverse, sems, own_sem, left, rounded, left_sems, half_sem = rest[-14:]
    sub_rows, slots, keeps = dims
    count = sub_rows * keeps
    layer = lax.axis_index("layer")
    start = layer * there.shape[0] + first
    loads = []
    for row in range(sub_rows):
        for at, blocks in enumerate((here.at[start + row], there.at[first + row])):
            loads.append(
                pltpu.make_async_copy(
                    blocks, left.at[pl.ds((2 * row + at) * slots, slots)], left_sems.at[2 * row + at]
                )
            )
    for load in loads:
        load.start()
    acc[...] = jnp.zeros_like(acc)
    found = (l1, l2, l3)
    total = listed(dims, left_cols, cols, keep, left, found, inverse)
    for load in loads:
        load.wait()
    multiply(total, lambda at: left[at], right, acc, count, found, buffers, sems)
    save = pltpu.make_async_copy(acc.at[pl.ds(0, count)], out, own_sem)
    save.start()

    def finish(at):
        rounded[at] = acc[at].astype(rounded.dtype)

    each_block(count, finish)
    send = pltpu.make_async_copy(rounded, half, half_sem)
    send.start()
    send.wait()
    save.wait()


def cube_here_kernel(
    dims, left_cols, cols, keep, blocks, right, base, *rest
):
    out, acc, buffers, l1, l2, l3, inverse, sems, own_sem, left, left_sem = rest[-11:]
    count = dims[0] * dims[2]
    fetch = pltpu.make_async_copy(blocks, left, left_sem)
    fetch.start()
    load = pltpu.make_async_copy(base, acc.at[pl.ds(0, count)], own_sem)
    load.start()
    found = (l1, l2, l3)
    total = listed(dims, left_cols, cols, keep, left, found, inverse)
    load.wait()
    fetch.wait()

    def begin(at):
        acc[at] = -1.5 * acc[at]

    each_block(count, begin)
    multiply(total, lambda at: left[at], right, acc, count, found, buffers, sems)
    save = pltpu.make_async_copy(acc.at[pl.ds(0, count)], out, own_sem)
    save.start()
    save.wait()


def cube_there_kernel(
    dims, first, left_cols, cols, keep, blocks, right, base, *rest
):
    out, acc, buffers, l1, l2, l3, inverse, sems, own_sem, left, left_sem, done = rest[-12:]
    count = dims[0] * dims[2]
    fetch = pltpu.make_async_copy(blocks, left, left_sem)
    fetch.start()
    load = pltpu.make_async_copy(base, acc.at[pl.ds(0, count)], own_sem)
    load.start()
    found = (l1, l2, l3)
    total = listed(dims, left_cols, cols, keep, left, found, inverse)
    load.wait()
    fetch.wait()
    multiply(total, lambda at: left[at], right, acc, count, found, buffers, sems)

    def finish(at):
        done[at] = (-2.0 * acc[at]).astype(done.dtype)

    each_block(count, finish)
    save = pltpu.make_async_copy(done, out.at[pl.ds(first, count)], own_sem)
    save.start()
    save.wait()


def products(kernel, outs, dims, left_cols, cols, keep, left, right, extra, width, name, more=(), alias=None):
    sub_rows, slots, keeps = dims
    block = right.shape[1:]
    count = sub_rows * keeps
    entries = left_cols.shape[0] * slots + GROUP
    smem = pl.BlockSpec(memory_space=pltpu.SMEM)
    vmem = pl.BlockSpec(memory_space=pltpu.VMEM)
    hbm = pl.BlockSpec(memory_space=pltpu.HBM)
    scalars = pltpu.SMEM((entries,), jnp.int32)
    return pl.pallas_call(
        kernel,
        out_shape=tuple(jax.ShapeDtypeStruct((n,) + block, t) for n, t, place in outs),
        in_specs=[smem] * 3 + [hbm] * (len(left) + 1 + len(extra)),
        out_specs=tuple({"vmem": vmem, "hbm": hbm}[place] for n, t, place in outs),
        scratch_shapes=[
            pltpu.VMEM((count + 1,) + block, jnp.float32),
            pltpu.VMEM((DEPTH,) + block, right.dtype),
            scalars,
            scalars,
            scalars,
            pltpu.SMEM((sub_rows * width,), jnp.int32),
            pltpu.SemaphoreType.DMA((DEPTH,)),
            pltpu.SemaphoreType.DMA,
            *more,
        ],
        input_output_aliases={} if alias is None else {alias: 0},
        compiler_params=pltpu.CompilerParams(vmem_limit_bytes=64 * 1024 * 1024),
        cost_estimate=pl.CostEstimate(
flops=1000, bytes_accessed=1000, transcendentals=0
        ),
        name=name,
    )(left_cols, cols, keep, *left, right, *extra)


def shards(p_blocks, p_cols, keep_cols):
    n_row = lax.axis_size("row")
    layer = lax.axis_index("layer")
    rows, slots = p_blocks.shape[:2]
    block = p_blocks.shape[2:]
    keeps = keep_cols.shape[1]
    sub_rows = rows // lax.axis_size("layer")
    width = n_row * rows

    unused = jnp.zeros((rows, LANES - slots - keeps), jnp.int32)
    meta = jnp.concatenate([p_cols, keep_cols, unused], axis=1)
    full, table, other_blocks, other_meta = gather(p_blocks, meta, n_row)

    def own(values):
        return lax.dynamic_slice_in_dim(values, layer * sub_rows, sub_rows, 0)

    right = full.reshape((width * slots,) + block)
    cols = table[:, :, :slots].reshape(-1)
    meta_here, meta_there = own(meta), own(other_meta)
    tail = max(sub_rows // 4, 1)
    middle = (sub_rows - 2 * tail) // 2
    cuts = (0, tail, sub_rows - tail, sub_rows)
    lots = [(lo, hi) for lo, hi in zip(cuts[:-1], cuts[1:]) if hi > lo]
    f32, bf16 = jnp.float32, jnp.bfloat16
    state = []
    for lo, hi in lots:
        dims = (hi - lo, slots, keeps)
        count = (hi - lo) * keeps
        here, there = meta_here[lo:hi], meta_there[lo:hi]
        keep_here = here[:, slots : slots + keeps].reshape(-1)
        keep_there = there[:, slots : slots + keeps].reshape(-1)
        left_cols = jnp.concatenate([here[:, :slots], there[:, :slots]], axis=1).reshape(-1)
        square, half = products(
            functools.partial(square_kernel, dims, lo),
            ((count, f32, "hbm"), (count, bf16, "hbm")),
            dims,
            left_cols,
            cols,
            keep_here,
            (p_blocks, other_blocks),
            right,
            tuple(entry[4] for entry in state[-1:]) + tuple(entry[-1] for entry in state[:-1]),
            width,
            f"square_{lo}",
            (
                pltpu.VMEM(((hi - lo) * 2 * slots,) + block, bf16),
                pltpu.VMEM((count,) + block, bf16),
                pltpu.SemaphoreType.DMA(((hi - lo) * 2,)),
                pltpu.SemaphoreType.DMA,
            ),
        )
        half_there = lax.ppermute(half, "col", [(0, 1), (1, 0)])
        state.append((lo, dims, keep_here, keep_there, square, half, half_there))
    partials = []
    for lo, dims, keep_here, keep_there, square, half, half_there in state:
        (partial,) = products(
            functools.partial(cube_here_kernel, dims),
            ((half.shape[0], f32, "hbm"),),
            dims,
            keep_here,
            cols,
            keep_here,
            (half,),
            right,
            (square,),
            width,
            f"cube_here_{lo}",
            (pltpu.VMEM(half.shape, bf16), pltpu.SemaphoreType.DMA),
        )
        partials.append(partial)
    result = None
    for partial, (lo, dims, keep_here, keep_there, square, half, half_there) in zip(partials, state):
        (result,) = products(
            functools.partial(cube_there_kernel, dims, lo * keeps),
            ((sub_rows * keeps, bf16, "hbm"),),
            dims,
            keep_there,
            cols,
            keep_here,
            (half_there,),
            right,
            (partial,) + (() if result is None else (result,)),
            width,
            f"cube_there_{lo}",
            (pltpu.VMEM(half.shape, bf16), pltpu.SemaphoreType.DMA, pltpu.VMEM(half.shape, bf16)),
            None if result is None else 6,
        )
    return result.reshape((sub_rows, keeps) + block)


def solution(mesh):
    placed = (P("row", "col", None, None), P("row", "col"), P("row", "col"))
    return jax.shard_map(
        shards,
        mesh=mesh,
        in_specs=placed,
        out_specs=P(("row", "layer"), "col", None, None),
        check_vma=False,
    )
```
